32 devices in a mesh: grp: 4 (over y, x), dev: 8 (over z, core).
Axes of the slice: x: 2, y: 2, z: 4, core: 2. Of those that a mesh axis runs over, the one named last changes fastest.
Arguments:
- amplitudes: float32 [2, 4, 8, 8192], P(None, 'grp', 'dev'), may hold values from -6 to 6
- joined_gates: float32 [4, 2, 128, 128], replicated, may hold values from -0.375 to 0.375
- pair_gate: float32 [2, 4, 4], replicated, may hold values from -2 to 2
- layout_in: int32 [18], replicated, may hold values from 0 to 17, as said below
- layout_out: int32 [18], replicated, may hold values from 0 to 17, as said below
- gate_qubits: int32 [4, 7], replicated, may hold values from 0 to 17, as said below
- spare_values: int32 [10], replicated, may hold values from 0 to 1
Outputs:
- evolved: float32 [2, 4, 8, 8192], P(None, 'grp', 'dev')
The draws below stay inside these ranges and needn't reach their ends.
Inputs may be any that keep to these rules, and one draw needn't show every extreme that they name: `layout_in`: a permutation of the qubits. `layout_out`: a permutation of the qubits; entries 13 + 3 onward equal those of layout_in; entries 13 to 15 are qubits that layout_in holds below position 13. `gate_qubits`: each row holds 7 different qubits; rows 0 and 1 name qubits that layout_in holds below position 13, rows 2 and 3 qubits that layout_out holds below position 13.
All inputs are finite; a program needn't handle non-finite values.
Results may differ from the reference program's by a relative error of at most 0.0001.
Values sent between devices are 32-bit elements; how exact they have to be, the bound alone decides.
A program may use at most 64 MiB of HBM per device.

```python
import jax
import jax.numpy as jnp
from jax import lax

AMPS = 8192
GATES = 4
GATE_QUBITS = 7
SPARE = 10
SPAN = 128
LQ = 13
DQ = 3
GQ = 2
N_GRP = 4
N_DEV = 8


def layouts(key):
    base_key = jax.random.fold_in(key, 4099)
    subkeys = jax.random.split(base_key, 7)
    qubit_count = LQ + DQ + GQ
    layout_in = jax.random.permutation(subkeys[0], qubit_count).astype(jnp.int32)
    local_in = layout_in[:LQ]
    shuffled = jax.random.permutation(subkeys[1], local_in)
    leaving = shuffled[:DQ]
    staying = jnp.concatenate([shuffled[DQ:], layout_in[LQ:LQ + DQ]])
    local_out = jax.random.permutation(subkeys[2], staying)
    layout_out = jnp.concatenate([local_out, leaving, layout_in[LQ + DQ:]]).astype(jnp.int32)
    gate_rows = []
    for gate_num in range(4):
        source_set = local_in if gate_num < 2 else local_out
        gate_rows.append(jax.random.permutation(subkeys[3 + gate_num], source_set)[:GATE_QUBITS])
    return (layout_in, layout_out, jnp.stack(gate_rows).astype(jnp.int32))


def draw_layout_in(key, part):
    return layouts(key)[0]


def draw_layout_out(key, part):
    return layouts(key)[1]


def draw_gate_qubits(key, part):
    return layouts(key)[2]


def plant(values, stream_key, least, high):
    shape = values.shape
    spot = [jax.random.randint(jax.random.fold_in(stream_key, axis), (), 0, shape[axis]) for axis in range(len(shape))]
    values = values.at[tuple(spot)].set(least)
    longest = shape.index(max(shape))
    spot[longest] = (spot[longest] + 1) % shape[longest]
    return values.at[tuple(spot)].set(high)


def block_levels(own_key, dims, cuts, smallest, top_value):
    level = 1.0
    for axis_at, blocks in cuts:
        steps = jax.random.uniform(jax.random.fold_in(jax.random.fold_in(own_key, 6), axis_at), (blocks,), jnp.float32, smallest / len(cuts), top_value / len(cuts))
        level = level * jnp.repeat(jnp.exp(steps), dims[axis_at] // blocks).reshape((-1,) + (1,) * (len(dims) - 1 - axis_at))
    return level


def normal_values(stream_key, dims, scale, reach, cuts=(), kind=jnp.bfloat16):
    array = jax.random.normal(stream_key, dims, jnp.float32) * scale
    if len(cuts) > 0:
        array = block_levels(stream_key, dims, cuts, -0.22, 0.18) * array
    return jnp.clip(array, min=-reach, max=reach).astype(kind)


def setup_inputs(seed: int = 0) -> dict:
    seeds = jax.random.split(jax.random.key(seed), 8)
    amplitudes = normal_values(seeds[0], (2, N_GRP, N_DEV, AMPS), 1.0, 6.0, ((1, 4), (2, 8)), jnp.float32)
    joined_gates = normal_values(seeds[1], (GATES, 2, SPAN, SPAN), (2 * SPAN) ** -0.5, 0.375, (), jnp.float32)
    pair_gate = normal_values(seeds[2], (2, 4, 4), 8 ** -0.5, 2.0, (), jnp.float32)
    layout_in = draw_layout_in(jax.random.fold_in(seeds[7], 71), 0)
    layout_out = draw_layout_out(jax.random.fold_in(seeds[7], 71), 0)
    gate_qubits = draw_gate_qubits(jax.random.fold_in(seeds[7], 71), 0)
    spare_values = plant(jax.random.randint(seeds[6], (SPARE,), 0, 2), jax.random.fold_in(seeds[6], 1), 0, 1).astype(jnp.int32)
    return dict(amplitudes=amplitudes, joined_gates=joined_gates, pair_gate=pair_gate, layout_in=layout_in, layout_out=layout_out, gate_qubits=gate_qubits, spare_values=spare_values)


HIGHEST = lax.Precision.HIGHEST


def source_index(bit_order, bit_count):
    position = jnp.arange(2 ** bit_count, dtype=jnp.int32)
    source = jnp.zeros((2 ** bit_count,), jnp.int32)
    for place_bit in range(bit_count):
        source = source + jnp.left_shift(jnp.right_shift(position, place_bit) & 1, bit_order[place_bit])
    return source


def complex_gate(values, matrix):
    real_part = jnp.dot(values[0], matrix[0].T, precision=HIGHEST, preferred_element_type=jnp.float32) - jnp.dot(values[1], matrix[1].T, precision=HIGHEST, preferred_element_type=jnp.float32)
    imag_part = jnp.dot(values[0], matrix[1].T, precision=HIGHEST, preferred_element_type=jnp.float32) + jnp.dot(values[1], matrix[0].T, precision=HIGHEST, preferred_element_type=jnp.float32)
    return jnp.stack([real_part, imag_part])


def pair_apply(values, pos_a, pos_c, matrix):
    count_all = values.shape[1]
    lower_pos = min(pos_a, pos_c)
    upper_pos = max(pos_a, pos_c)
    shaped = values.reshape(2, count_all >> (upper_pos + 1), 2, 1 << (upper_pos - lower_pos - 1), 2, 1 << lower_pos)
    tensor = matrix.reshape(2, 2, 2, 2, 2)
    pattern = "uvwx,hwmxl->humvl" if pos_a < pos_c else "uvwx,hxmwl->hvmul"
    real_part = jnp.einsum(pattern, tensor[0], shaped[0], precision=HIGHEST) - jnp.einsum(pattern, tensor[1], shaped[1], precision=HIGHEST)
    imag_part = jnp.einsum(pattern, tensor[1], shaped[0], precision=HIGHEST) + jnp.einsum(pattern, tensor[0], shaped[1], precision=HIGHEST)
    return jnp.stack([real_part, imag_part]).reshape(2, count_all)


def spare_sign(count_all, spare_values):
    position = jnp.arange(count_all, dtype=jnp.int32)
    parity = jnp.zeros((count_all,), jnp.int32)
    for place_bit in range(spare_values.shape[0]):
        parity = parity + spare_values[place_bit] * (jnp.right_shift(position, place_bit) & 1)
    return (1 - 2 * (parity & 1)).astype(jnp.float32)


def reference(amplitudes, joined_gates, pair_gate, layout_in, layout_out, gate_qubits, spare_values):
    qubit_count = LQ + DQ + GQ
    flat_values = amplitudes.reshape(2, -1)
    qubit_ids = jnp.arange(qubit_count, dtype=jnp.int32)
    inverse_in = jnp.zeros((qubit_count,), jnp.int32).at[layout_in].set(qubit_ids)
    logical = jnp.take(flat_values, source_index(inverse_in, qubit_count), axis=1)
    for gate_num in range(GATES):
        chosen = gate_qubits[gate_num]
        member = qubit_ids[:, None] == chosen[None, :]
        inside = jnp.any(member, axis=1)
        others = jnp.logical_not(inside).astype(jnp.int32)
        inner_rank = jnp.sum(member * jnp.arange(chosen.shape[0], dtype=jnp.int32)[None, :], axis=1)
        target = jnp.where(inside, inner_rank, chosen.shape[0] + jnp.cumsum(others) - 1).astype(jnp.int32)
        bit_order = jnp.zeros((qubit_count,), jnp.int32).at[target].set(qubit_ids)
        arranged = jnp.take(logical, source_index(bit_order, qubit_count), axis=1)
        arranged = complex_gate(arranged.reshape(2, -1, SPAN), joined_gates[gate_num]).reshape(2, -1)
        logical = jnp.take(arranged, source_index(target, qubit_count), axis=1)
    stored = jnp.take(logical, source_index(layout_out, qubit_count), axis=1)
    stored = stored * spare_sign(stored.shape[1], spare_values)
    for bit_num in range(GQ):
        stored = pair_apply(stored, LQ + DQ + bit_num, LQ - 1 - bit_num, pair_gate)
    return stored.reshape(amplitudes.shape)
```

```python
import functools

import jax
import jax.numpy as jnp
from jax import lax
from jax.experimental import pallas as pl
from jax.experimental.pallas import tpu as pltpu
from jax.sharding import PartitionSpec as P

MESH = pl.DeviceIdType.MESH
LANE_BITS = 7
SUB_BITS = 3


def bits_of(size):
    return size.bit_length() - 1


def split(x):
    high = x.astype(jnp.bfloat16)
    low = (x - high.astype(jnp.float32)).astype(jnp.bfloat16)
    return high, low


def nt_dot(a, b):
    return lax.dot_general(
        a, b, (((1,), (1,)), ((), ())), preferred_element_type=jnp.float32
    )


def nn_dot(a, b):
    return jnp.dot(a, b, preferred_element_type=jnp.float32)


def plan(in_lane, load):
    rows = len(in_lane) - LANE_BITS
    lane_shift, row_shift = [], []
    lanes_packed = rows_packed = shift = jnp.int32(0)
    for j in range(LANE_BITS):
        out = 1 - in_lane[j]
        lanes_packed = lanes_packed | jnp.left_shift(out * j, shift)
        lane_shift.append(shift)
        shift = shift + 4 * out
    shift = jnp.int32(0)
    for r in range(rows):
        moved = in_lane[LANE_BITS + r]
        rows_packed = rows_packed | jnp.left_shift(moved * r, shift)
        row_shift.append(shift)
        shift = shift + 4 * moved
    row_coef, row_layout = [], []
    for r in range(rows):
        moved = in_lane[LANE_BITS + r]
        partner = jnp.right_shift(lanes_packed, row_shift[r]) & 15
        row_coef.append(jnp.left_shift(moved, partner) & (2**LANE_BITS - 1))
        row_layout.append(load(jnp.where(moved == 1, jnp.minimum(partner, LANE_BITS - 1), LANE_BITS + r)))
    lane_coef, lane_layout = [], []
    for j in range(LANE_BITS):
        out = 1 - in_lane[j]
        partner = jnp.right_shift(rows_packed, lane_shift[j]) & 15
        lane_coef.append(jnp.left_shift(out, partner) & (2**rows - 1))
        lane_layout.append(load(jnp.where(out == 1, LANE_BITS + jnp.minimum(partner, rows - 1), j)))
    return row_coef, lane_coef, row_layout, lane_layout


def place_of(qubit, layout):
    found = jnp.int32(0)
    for p in range(1, len(layout)):
        found = found + jnp.where(layout[p] == qubit, p, 0)
    return found


def qubit_set(qubits):
    mask = jnp.int32(0)
    for q in qubits:
        mask = mask | jnp.left_shift(jnp.int32(1), q)
    return mask


def kernel(
    n_grp,
    n_dev,
    halves,
    amp_ref,
    gates_ref,
    pair_ref,
    lin_ref,
    lout_ref,
    gq_ref,
    spare_ref,
    out_ref,
    lay_ref,
    send_ref,
    recv_ref,
    gsend_ref,
    grecv_ref,
    dsend_sem,
    drecv_sem,
    gsend_sem,
    grecv_sem,
):
    grp, dev = lax.axis_index("grp"), lax.axis_index("dev")
    gb, db = bits_of(n_grp), bits_of(n_dev)
    n_rows = amp_ref.shape[1]
    row_bits = bits_of(n_rows)
    local = row_bits + LANE_BITS
    tiles = n_rows // 8
    tile_bits = row_bits - SUB_BITS

    barrier = pltpu.get_barrier_semaphore()
    for off in range(1, n_dev):
        pl.semaphore_signal(barrier, inc=1, device_id=(grp, dev ^ off), device_id_type=MESH)
    for k in range(gb):
        pl.semaphore_signal(
            barrier, inc=1, device_id=(grp ^ (1 << k), dev), device_id_type=MESH
        )

    lane = lax.broadcasted_iota(jnp.int32, (8, 128), 1)
    sub = lax.broadcasted_iota(jnp.int32, (8, 128), 0)
    lane_mask = [-(jnp.right_shift(lane, j) & 1) for j in range(LANE_BITS)]
    sub_mask = [-(jnp.right_shift(sub, j) & 1) for j in range(SUB_BITS)]

    def combine(masks, coefs):
        total = masks[0] & coefs[0]
        for m, c in zip(masks[1:], coefs[1:]):
            total = total ^ (m & c)
        return total

    def take(x, idx, axis):
        return jnp.take_along_axis(x, idx, axis=axis, mode="promise_in_bounds")

    def shear(x, row_coef, lane_coef, order):
        sub_part = combine(sub_mask, row_coef[:SUB_BITS])
        tile_part = []
        for v in range(tiles):
            part = jnp.int32(0)
            for i in range(tile_bits):
                if v >> i & 1:
                    part = part ^ row_coef[SUB_BITS + i]
            tile_part.append(part)
        first = lane ^ sub_part
        x = [[take(t[v], first ^ tile_part[v], 1) for v in range(tiles)] for t in x]
        rows = combine(lane_mask, lane_coef)
        for i in range(tile_bits):
            cond = (jnp.right_shift(rows, SUB_BITS + i) & 1) == 1
            x = [[jnp.where(cond, t[v ^ (1 << i)], t[v]) for v in range(tiles)] for t in x]
        subs = sub ^ (rows & 7)
        x = [[take(t[v], subs, 0) for v in range(tiles)] for t in x]
        last = sub_part ^ (lane if order is None else combine(lane_mask, order))
        return [[take(t[v], last ^ tile_part[v], 1) for v in range(tiles)] for t in x]

    def to_matrix(x):
        return jnp.concatenate(
            [jnp.concatenate(t, axis=0) for t in x], axis=1
        )

    def to_tiles(y):
        return [
            [y[8 * v : 8 * v + 8, 128 * c : 128 * c + 128] for v in range(tiles)]
            for c in range(2)
        ]

    def gate_plan(layout, slot, qubits):
        for p in range(local):
            lay_ref[slot, p] = layout[p]
        mask = qubit_set(qubits)
        in_lane = [jnp.right_shift(mask, layout[p]) & 1 for p in range(local)]
        rc, lc, row_layout, lane_layout = plan(in_lane, lambda i: lay_ref[slot, i])
        order = [
            jnp.left_shift(jnp.int32(1), place_of(q, lane_layout)) & (2**LANE_BITS - 1)
            for q in qubits
        ]
        return rc, lc, order, list(qubits) + row_layout

    def gate(x, g):
        u_re, u_im = gates_ref[g, 0], gates_ref[g, 1]
        w = jnp.concatenate(
            [
                jnp.concatenate([u_re, -u_im], axis=1),
                jnp.concatenate([u_im, u_re], axis=1),
            ],
            axis=0,
        )
        w_high, w_low = split(w)
        high, low = split(to_matrix(x))
        both = nt_dot(jnp.concatenate([high, low], axis=0), w_high)
        y = both[:n_rows] + (both[n_rows:] + nt_dot(high, w_low))
        return to_tiles(y)

    def row_permute(x, source):
        r_out = lax.broadcasted_iota(jnp.int32, (n_rows, n_rows), 0)
        r_in = lax.broadcasted_iota(jnp.int32, (n_rows, n_rows), 1)
        want = jnp.zeros_like(r_out)
        for i in range(row_bits):
            want = want | jnp.left_shift(jnp.right_shift(r_out, i) & 1, source[i])
        pick = jnp.where(want == r_in, 1.0, 0.0).astype(jnp.bfloat16)
        high, low = split(to_matrix(x))
        y = nn_dot(pick, jnp.concatenate([high, low], axis=1))
        return y[:, :256] + y[:, 256:]

    layout = [lin_ref[p] for p in range(local)]
    x = [[amp_ref[c, 8 * v : 8 * v + 8] for v in range(tiles)] for c in range(2)]
    for g in range(2):
        rc, lc, order, layout = gate_plan(layout, g, [gq_ref[g, i] for i in range(LANE_BITS)])
        x = gate(shear(x, rc, lc, order), g)

    leaving = [lout_ref[local + i] for i in range(db)]
    for p in range(local):
        lay_ref[2, p] = layout[p]
    mask = qubit_set(leaving)
    count = jnp.int32(0)
    in_lane = []
    for p in range(local):
        stays = 1 - (jnp.right_shift(mask, layout[p]) & 1)
        stays = jnp.where(count < LANE_BITS, stays, 0)
        in_lane.append(stays)
        count = count + stays
    rc, lc, row_layout, lane_layout = plan(in_lane, lambda i: lay_ref[2, i])
    packed = rank = jnp.int32(0)
    for r in range(row_bits):
        stays = 1 - (jnp.right_shift(mask, row_layout[r]) & 1)
        packed = packed | jnp.left_shift(stays * r, rank)
        rank = rank + 4 * stays
    for r in range(row_bits):
        lay_ref[3, r] = row_layout[r]
    source = [jnp.right_shift(packed, 4 * i) & 15 for i in range(row_bits - db)]
    stay_rows = [lay_ref[3, jnp.minimum(s, row_bits - 1)] for s in source]
    source = source + [place_of(q, row_layout) for q in leaving]
    y = row_permute(shear(x, rc, lc, None), source)
    layout = lane_layout + stay_rows + [lin_ref[local + i] for i in range(db)]

    depth = n_rows // n_dev
    for c in range(2):
        send_ref[:, c * depth : (c + 1) * depth, :] = y[:, 128 * c : 128 * c + 128].reshape(
            n_dev, depth, 128
        )
    recv_ref[dev] = send_ref[dev]

    pl.semaphore_wait(barrier, n_dev - 1 + gb)
    copies = []
    for off in range(n_dev - 1, 0, -1):
        copy = pltpu.make_async_remote_copy(
            src_ref=send_ref.at[dev ^ off],
            dst_ref=recv_ref.at[dev],
            send_sem=dsend_sem.at[off],
            recv_sem=drecv_sem.at[off],
            device_id=(grp, dev ^ off),
            device_id_type=MESH,
        )
        copy.start()
        copies.append(copy)

    rc, lc, order, layout = gate_plan(layout, 4, [gq_ref[2, i] for i in range(LANE_BITS)])
    for copy in copies:
        copy.wait_recv()
    x = []
    for c in range(2):
        flat = recv_ref[:, c * depth : (c + 1) * depth, :].reshape(n_rows, 128)
        x.append([flat[8 * v : 8 * v + 8] for v in range(tiles)])
    x = gate(shear(x, rc, lc, order), 2)
    rc, lc, order, layout = gate_plan(layout, 5, [gq_ref[3, i] for i in range(LANE_BITS)])
    x = gate(shear(x, rc, lc, order), 3)
    rc, lc, order, layout = gate_plan(layout, 6, [lout_ref[i] for i in range(LANE_BITS)])
    source = [place_of(lout_ref[LANE_BITS + i], layout[LANE_BITS:]) for i in range(row_bits)]
    y = row_permute(shear(x, rc, lc, order), source)

    spare = spare_ref.shape[0]
    flip = combine(lane_mask, [spare_ref[i] & 1 for i in range(min(spare, LANE_BITS))])
    position = lax.broadcasted_iota(jnp.int32, (n_rows, 128), 0)
    flip = jnp.concatenate([flip] * tiles, axis=0)
    for i in range(LANE_BITS, spare):
        flip = flip ^ (jnp.right_shift(position, i - LANE_BITS) & spare_ref[i] & 1)
    sign = (1 - 2 * (flip & 1)).astype(jnp.float32)
    x = to_tiles(y * jnp.concatenate([sign, sign], axis=1))

    def coefficient(c, row, col):
        return pair_ref[c, row, col]

    def pair_gate(own, other, k, names):
        a = jnp.right_shift(grp, k) & 1
        row_bit = row_bits - 1 - k
        if row_bit >= SUB_BITS:
            step = 1 << (row_bit - SUB_BITS)
            flipped = lambda t, v: t[v ^ step]
        else:
            step = 1 << row_bit
            flipped = lambda t, v: (
                jnp.where(
                    (sub & step) == 0, pltpu.roll(t[v], 8 - step, 0), pltpu.roll(t[v], step, 0)
                )
            )
        weights = {}
        for cbit in range(2):
            for src in range(2):
                for cs in range(2):
                    col = (a if src == 0 else 1 - a) + 2 * (cbit if cs == 0 else 1 - cbit)
                    weights[cbit, src, cs] = [
                        coefficient(part, a + 2 * cbit, col) for part in range(2)
                    ]
        out = [{}, {}]
        for v in names:
            re = im = None
            for src, data in enumerate((own, other)):
                for cs in range(2):
                    if row_bit >= SUB_BITS:
                        cbit = v >> (row_bit - SUB_BITS) & 1
                        w_re, w_im = weights[cbit, src, cs]
                    else:
                        high = (sub & step) != 0
                        w_re, w_im = [
                            jnp.where(high, weights[1, src, cs][p], weights[0, src, cs][p])
                            for p in range(2)
                        ]
                    d_re, d_im = [
                        data[c][v] if cs == 0 else flipped(data[c], v) for c in range(2)
                    ]
                    t_re = w_re * d_re - w_im * d_im
                    t_im = w_im * d_re + w_re * d_im
                    re = t_re if re is None else re + t_re
                    im = t_im if im is None else im + t_im
            out[0][v], out[1][v] = re, im
        return out

    groups = [[v for v in range(tiles) if v % halves == h] for h in range(halves)]
    held = [[{v: x[c][v] for v in names} for c in range(2)] for names in groups]
    count = tiles // halves
    pending = []
    for phase in range(gb):
        started = []
        for h, names in enumerate(groups):
            k = phase if h == 0 else gb - 1 - phase
            for c in range(2):
                for n, v in enumerate(names):
                    gsend_ref[phase, h, c, 8 * n : 8 * n + 8, :] = held[h][c][v]
            copy = pltpu.make_async_remote_copy(
                src_ref=gsend_ref.at[phase, h],
                dst_ref=grecv_ref.at[phase, h],
                send_sem=gsend_sem.at[phase, h],
                recv_sem=grecv_sem.at[phase, h],
                device_id=(grp ^ (1 << k), dev),
                device_id_type=MESH,
            )
            copy.start()
            started.append((h, names, k, copy))
        for h, names, k, copy in started:
            copy.wait_recv()
            other = [
                {v: grecv_ref[phase, h, c, 8 * n : 8 * n + 8, :] for n, v in enumerate(names)}
                for c in range(2)
            ]
            held[h] = pair_gate(held[h], other, k, names)
            pending.append(copy)
    for names, part in zip(groups, held):
        for c in range(2):
            for v in names:
                out_ref[c, 8 * v : 8 * v + 8, :] = part[c][v]
    for copy in copies + pending:
        copy.wait_send()


def per_device(
    amplitudes, joined_gates, pair_gate, layout_in, layout_out, gate_qubits, spare_values
):
    n_grp, n_dev = lax.axis_size("grp"), lax.axis_size("dev")
    gb = bits_of(n_grp)
    n_rows = amplitudes.shape[-1] // 128
    tiles = n_rows // 8
    halves = 2 if gb == 2 else 1
    values = amplitudes.reshape(2, n_rows, 128)
    vmem = pl.BlockSpec(memory_space=pltpu.VMEM)
    smem = pl.BlockSpec(memory_space=pltpu.SMEM)
    depth = n_rows // n_dev
    out = pl.pallas_call(
        functools.partial(kernel, n_grp, n_dev, halves),
        out_shape=jax.ShapeDtypeStruct(values.shape, jnp.float32),
        in_specs=[vmem, vmem, smem, smem, smem, smem, smem],
        out_specs=vmem,
        scratch_shapes=[
            pltpu.SMEM((8, 16), jnp.int32),
            pltpu.VMEM((n_dev, 2 * depth, 128), jnp.float32),
            pltpu.VMEM((n_dev, 2 * depth, 128), jnp.float32),
            pltpu.VMEM((gb, halves, 2, n_rows // halves, 128), jnp.float32),
            pltpu.VMEM((gb, halves, 2, n_rows // halves, 128), jnp.float32),
            pltpu.SemaphoreType.DMA((n_dev,)),
            pltpu.SemaphoreType.DMA((n_dev,)),
            pltpu.SemaphoreType.DMA((gb, halves)),
            pltpu.SemaphoreType.DMA((gb, halves)),
        ],
        compiler_params=pltpu.CompilerParams(
            collective_id=0, has_side_effects=True, vmem_limit_bytes=32 * 1024 * 1024
        ),
    )(values, joined_gates, pair_gate, layout_in, layout_out, gate_qubits, spare_values)
    return out.reshape(amplitudes.shape)


def solution(mesh):
    in_specs = (P(None, "grp", "dev", None), P(), P(), P(), P(), P(), P())
    out_specs = P(None, "grp", "dev", None)
    return jax.shard_map(
        per_device, mesh=mesh, in_specs=in_specs, out_specs=out_specs, check_vma=False
    )
```

```python
import functools

import jax
import jax.numpy as jnp
from jax import lax
from jax.experimental import pallas as pl
from jax.experimental.pallas import tpu as pltpu
from jax.sharding import PartitionSpec as P

MESH = pl.DeviceIdType.MESH
LANE_BITS = 7
SUB_BITS = 3


def bits_of(size):
    return size.bit_length() - 1


def split(x):
    high = x.astype(jnp.bfloat16)
    low = (x - high.astype(jnp.float32)).astype(jnp.bfloat16)
    return high, low


def nt_dot(a, b):
    return lax.dot_general(
        a, b, (((1,), (1,)), ((), ())), preferred_element_type=jnp.float32
    )


def nn_dot(a, b):
    return jnp.dot(a, b, preferred_element_type=jnp.float32)


def plan(in_lane, load):
    rows = len(in_lane) - LANE_BITS
    lane_shift, row_shift = [], []
    lanes_packed = rows_packed = shift = jnp.int32(0)
    for j in range(LANE_BITS):
        out = 1 - in_lane[j]
        lanes_packed = lanes_packed | jnp.left_shift(out * j, shift)
        lane_shift.append(shift)
        shift = shift + 4 * out
    shift = jnp.int32(0)
    for r in range(rows):
        moved = in_lane[LANE_BITS + r]
        rows_packed = rows_packed | jnp.left_shift(moved * r, shift)
        row_shift.append(shift)
        shift = shift + 4 * moved
    row_coef, row_layout = [], []
    for r in range(rows):
        moved = in_lane[LANE_BITS + r]
        partner = jnp.right_shift(lanes_packed, row_shift[r]) & 15
        row_coef.append(jnp.left_shift(moved, partner) & (2**LANE_BITS - 1))
        row_layout.append(load(jnp.where(moved == 1, jnp.minimum(partner, LANE_BITS - 1), LANE_BITS + r)))
    lane_coef, lane_layout = [], []
    for j in range(LANE_BITS):
        out = 1 - in_lane[j]
        partner = jnp.right_shift(rows_packed, lane_shift[j]) & 15
        lane_coef.append(jnp.left_shift(out, partner) & (2**rows - 1))
        lane_layout.append(load(jnp.where(out == 1, LANE_BITS + jnp.minimum(partner, rows - 1), j)))
    return row_coef, lane_coef, row_layout, lane_layout


def place_of(qubit, layout):
    found = jnp.int32(0)
    for p in range(1, len(layout)):
        found = found + jnp.where(layout[p] == qubit, p, 0)
    return found


def qubit_set(qubits):
    mask = jnp.int32(0)
    for q in qubits:
        mask = mask | jnp.left_shift(jnp.int32(1), q)
    return mask


def kernel(
    n_grp,
    n_dev,
    halves,
    amp_ref,
    gates_hbm,
    pair_ref,
    lin_ref,
    lout_ref,
    gq_ref,
    spare_ref,
    out_ref,
    lay_ref,
    send_ref,
    recv_ref,
    gsend_ref,
    grecv_ref,
    dsend_sem,
    drecv_sem,
    gsend_sem,
    grecv_sem,
    gates_ref,
    gates_sem,
):
    fetches = [
        pltpu.make_async_copy(gates_hbm.at[g], gates_ref.at[g], gates_sem.at[g])
        for g in range(4)
    ]
    for fetch in fetches:
        fetch.start()
    grp, dev = lax.axis_index("grp"), lax.axis_index("dev")
    gb, db = bits_of(n_grp), bits_of(n_dev)
    n_rows = amp_ref.shape[1]
    row_bits = bits_of(n_rows)
    local = row_bits + LANE_BITS
    tiles = n_rows // 8
    tile_bits = row_bits - SUB_BITS

    barrier = pltpu.get_barrier_semaphore()
    for off in range(1, n_dev):
        pl.semaphore_signal(barrier, inc=1, device_id=(grp, dev ^ off), device_id_type=MESH)
    for k in range(gb):
        pl.semaphore_signal(
            barrier, inc=1, device_id=(grp ^ (1 << k), dev), device_id_type=MESH
        )

    lane = lax.broadcasted_iota(jnp.int32, (8, 128), 1)
    sub = lax.broadcasted_iota(jnp.int32, (8, 128), 0)
    lane_mask = [-(jnp.right_shift(lane, j) & 1) for j in range(LANE_BITS)]
    sub_mask = [-(jnp.right_shift(sub, j) & 1) for j in range(SUB_BITS)]

    def combine(masks, coefs):
        total = masks[0] & coefs[0]
        for m, c in zip(masks[1:], coefs[1:]):
            total = total ^ (m & c)
        return total

    def take(x, idx, axis):
        return jnp.take_along_axis(x, idx, axis=axis, mode="promise_in_bounds")

    def shear(x, row_coef, lane_coef, order):
        sub_part = combine(sub_mask, row_coef[:SUB_BITS])
        tile_part = []
        for v in range(tiles):
            part = jnp.int32(0)
            for i in range(tile_bits):
                if v >> i & 1:
                    part = part ^ row_coef[SUB_BITS + i]
            tile_part.append(part)
        first = lane ^ sub_part
        x = [[take(t[v], first ^ tile_part[v], 1) for v in range(tiles)] for t in x]
        rows = combine(lane_mask, lane_coef)
        for i in range(tile_bits):
            cond = (jnp.right_shift(rows, SUB_BITS + i) & 1) == 1
            x = [[jnp.where(cond, t[v ^ (1 << i)], t[v]) for v in range(tiles)] for t in x]
        subs = sub ^ (rows & 7)
        x = [[take(t[v], subs, 0) for v in range(tiles)] for t in x]
        last = sub_part ^ (lane if order is None else combine(lane_mask, order))
        return [[take(t[v], last ^ tile_part[v], 1) for v in range(tiles)] for t in x]

    def to_matrix(x):
        return jnp.concatenate(
            [jnp.concatenate(t, axis=0) for t in x], axis=1
        )

    def to_tiles(y):
        return [
            [y[8 * v : 8 * v + 8, 128 * c : 128 * c + 128] for v in range(tiles)]
            for c in range(2)
        ]

    def gate_plan(layout, slot, qubits):
        for p in range(local):
            lay_ref[slot, p] = layout[p]
        mask = qubit_set(qubits)
        in_lane = [jnp.right_shift(mask, layout[p]) & 1 for p in range(local)]
        rc, lc, row_layout, lane_layout = plan(in_lane, lambda i: lay_ref[slot, i])
        order = [
            jnp.left_shift(jnp.int32(1), place_of(q, lane_layout)) & (2**LANE_BITS - 1)
            for q in qubits
        ]
        return rc, lc, order, list(qubits) + row_layout

    def gate(x, g):
        fetches[g].wait()
        u_re, u_im = gates_ref[g, 0], gates_ref[g, 1]
        w = jnp.concatenate(
            [
                jnp.concatenate([u_re, -u_im], axis=1),
                jnp.concatenate([u_im, u_re], axis=1),
            ],
            axis=0,
        )
        w_high, w_low = split(w)
        high, low = split(to_matrix(x))
        both = nt_dot(jnp.concatenate([high, low], axis=0), w_high)
        y = both[:n_rows] + (both[n_rows:] + nt_dot(high, w_low))
        return to_tiles(y)

    def row_permute(x, source):
        r_out = lax.broadcasted_iota(jnp.int32, (n_rows, n_rows), 0)
        r_in = lax.broadcasted_iota(jnp.int32, (n_rows, n_rows), 1)
        want = jnp.zeros_like(r_out)
        for i in range(row_bits):
            want = want | jnp.left_shift(jnp.right_shift(r_out, i) & 1, source[i])
        pick = jnp.where(want == r_in, 1.0, 0.0).astype(jnp.bfloat16)
        high, low = split(to_matrix(x))
        y = nn_dot(pick, jnp.concatenate([high, low], axis=1))
        return y[:, :256] + y[:, 256:]

    layout = [lin_ref[p] for p in range(local)]
    x = [[amp_ref[c, 8 * v : 8 * v + 8] for v in range(tiles)] for c in range(2)]
    for g in range(2):
        rc, lc, order, layout = gate_plan(layout, g, [gq_ref[g, i] for i in range(LANE_BITS)])
        x = gate(shear(x, rc, lc, order), g)

    leaving = [lout_ref[local + i] for i in range(db)]
    for p in range(local):
        lay_ref[2, p] = layout[p]
    mask = qubit_set(leaving)
    count = jnp.int32(0)
    in_lane = []
    for p in range(local):
        stays = 1 - (jnp.right_shift(mask, layout[p]) & 1)
        stays = jnp.where(count < LANE_BITS, stays, 0)
        in_lane.append(stays)
        count = count + stays
    rc, lc, row_layout, lane_layout = plan(in_lane, lambda i: lay_ref[2, i])
    packed = rank = jnp.int32(0)
    for r in range(row_bits):
        stays = 1 - (jnp.right_shift(mask, row_layout[r]) & 1)
        packed = packed | jnp.left_shift(stays * r, rank)
        rank = rank + 4 * stays
    for r in range(row_bits):
        lay_ref[3, r] = row_layout[r]
    source = [jnp.right_shift(packed, 4 * i) & 15 for i in range(row_bits - db)]
    stay_rows = [lay_ref[3, jnp.minimum(s, row_bits - 1)] for s in source]
    source = source + [place_of(q, row_layout) for q in leaving]
    y = row_permute(shear(x, rc, lc, None), source)
    layout = lane_layout + stay_rows + [lin_ref[local + i] for i in range(db)]

    depth = n_rows // n_dev
    for c in range(2):
        send_ref[:, c * depth : (c + 1) * depth, :] = y[:, 128 * c : 128 * c + 128].reshape(
            n_dev, depth, 128
        )
    recv_ref[dev] = send_ref[dev]

    pl.semaphore_wait(barrier, n_dev - 1 + gb)
    copies = []
    for off in range(n_dev - 1, 0, -1):
        copy = pltpu.make_async_remote_copy(
            src_ref=send_ref.at[dev ^ off],
            dst_ref=recv_ref.at[dev],
            send_sem=dsend_sem.at[off],
            recv_sem=drecv_sem.at[off],
            device_id=(grp, dev ^ off),
            device_id_type=MESH,
        )
        copy.start()
        copies.append(copy)

    rc, lc, order, layout = gate_plan(layout, 4, [gq_ref[2, i] for i in range(LANE_BITS)])
    for copy in copies:
        copy.wait_recv()
    x = []
    for c in range(2):
        flat = recv_ref[:, c * depth : (c + 1) * depth, :].reshape(n_rows, 128)
        x.append([flat[8 * v : 8 * v + 8] for v in range(tiles)])
    x = gate(shear(x, rc, lc, order), 2)
    rc, lc, order, layout = gate_plan(layout, 5, [gq_ref[3, i] for i in range(LANE_BITS)])
    x = gate(shear(x, rc, lc, order), 3)
    rc, lc, order, layout = gate_plan(layout, 6, [lout_ref[i] for i in range(LANE_BITS)])
    source = [place_of(lout_ref[LANE_BITS + i], layout[LANE_BITS:]) for i in range(row_bits)]
    y = row_permute(shear(x, rc, lc, order), source)

    spare = spare_ref.shape[0]
    flip = combine(lane_mask, [spare_ref[i] & 1 for i in range(min(spare, LANE_BITS))])
    position = lax.broadcasted_iota(jnp.int32, (n_rows, 128), 0)
    flip = jnp.concatenate([flip] * tiles, axis=0)
    for i in range(LANE_BITS, spare):
        flip = flip ^ (jnp.right_shift(position, i - LANE_BITS) & spare_ref[i] & 1)
    sign = (1 - 2 * (flip & 1)).astype(jnp.float32)
    x = to_tiles(y * jnp.concatenate([sign, sign], axis=1))

    def coefficient(c, row, col):
        return pair_ref[c, row, col]

    def pair_gate(own, other, k, names):
        a = jnp.right_shift(grp, k) & 1
        row_bit = row_bits - 1 - k
        if row_bit >= SUB_BITS:
            step = 1 << (row_bit - SUB_BITS)
            flipped = lambda t, v: t[v ^ step]
        else:
            step = 1 << row_bit
            flipped = lambda t, v: (
                jnp.where(
                    (sub & step) == 0, pltpu.roll(t[v], 8 - step, 0), pltpu.roll(t[v], step, 0)
                )
            )
        weights = {}
        for cbit in range(2):
            for src in range(2):
                for cs in range(2):
                    col = (a if src == 0 else 1 - a) + 2 * (cbit if cs == 0 else 1 - cbit)
                    weights[cbit, src, cs] = [
                        coefficient(part, a + 2 * cbit, col) for part in range(2)
                    ]
        out = [{}, {}]
        for v in names:
            re = im = None
            for src, data in enumerate((own, other)):
                for cs in range(2):
                    if row_bit >= SUB_BITS:
                        cbit = v >> (row_bit - SUB_BITS) & 1
                        w_re, w_im = weights[cbit, src, cs]
                    else:
                        high = (sub & step) != 0
                        w_re, w_im = [
                            jnp.where(high, weights[1, src, cs][p], weights[0, src, cs][p])
                            for p in range(2)
                        ]
                    d_re, d_im = [
                        data[c][v] if cs == 0 else flipped(data[c], v) for c in range(2)
                    ]
                    t_re = w_re * d_re - w_im * d_im
                    t_im = w_im * d_re + w_re * d_im
                    re = t_re if re is None else re + t_re
                    im = t_im if im is None else im + t_im
            out[0][v], out[1][v] = re, im
        return out

    groups = [[v for v in range(tiles) if v % halves == h] for h in range(halves)]
    held = [[{v: x[c][v] for v in names} for c in range(2)] for names in groups]
    count = tiles // halves
    pending = []
    for phase in range(gb):
        started = []
        for h, names in enumerate(groups):
            k = phase if h == 0 else gb - 1 - phase
            for c in range(2):
                for n, v in enumerate(names):
                    gsend_ref[phase, h, c, 8 * n : 8 * n + 8, :] = held[h][c][v]
            copy = pltpu.make_async_remote_copy(
                src_ref=gsend_ref.at[phase, h],
                dst_ref=grecv_ref.at[phase, h],
                send_sem=gsend_sem.at[phase, h],
                recv_sem=grecv_sem.at[phase, h],
                device_id=(grp ^ (1 << k), dev),
                device_id_type=MESH,
            )
            copy.start()
            started.append((h, names, k, copy))
        for h, names, k, copy in started:
            copy.wait_recv()
            other = [
                {v: grecv_ref[phase, h, c, 8 * n : 8 * n + 8, :] for n, v in enumerate(names)}
                for c in range(2)
            ]
            held[h] = pair_gate(held[h], other, k, names)
            pending.append(copy)
    for names, part in zip(groups, held):
        for c in range(2):
            for v in names:
                out_ref[c, 8 * v : 8 * v + 8, :] = part[c][v]
    for copy in copies + pending:
        copy.wait_send()


def per_device(
    amplitudes, joined_gates, pair_gate, layout_in, layout_out, gate_qubits, spare_values
):
    n_grp, n_dev = lax.axis_size("grp"), lax.axis_size("dev")
    gb = bits_of(n_grp)
    n_rows = amplitudes.shape[-1] // 128
    tiles = n_rows // 8
    halves = 2 if gb == 2 else 1
    values = amplitudes.reshape(2, n_rows, 128)
    vmem = pl.BlockSpec(memory_space=pltpu.VMEM)
    smem = pl.BlockSpec(memory_space=pltpu.SMEM)
    depth = n_rows // n_dev
    out = pl.pallas_call(
        functools.partial(kernel, n_grp, n_dev, halves),
        out_shape=jax.ShapeDtypeStruct(values.shape, jnp.float32),
        in_specs=[vmem, pl.BlockSpec(memory_space=pl.ANY), smem, smem, smem, smem, smem],
        out_specs=vmem,
        scratch_shapes=[
            pltpu.SMEM((8, 16), jnp.int32),
            pltpu.VMEM((n_dev, 2 * depth, 128), jnp.float32),
            pltpu.VMEM((n_dev, 2 * depth, 128), jnp.float32),
            pltpu.VMEM((gb, halves, 2, n_rows // halves, 128), jnp.float32),
            pltpu.VMEM((gb, halves, 2, n_rows // halves, 128), jnp.float32),
            pltpu.SemaphoreType.DMA((n_dev,)),
            pltpu.SemaphoreType.DMA((n_dev,)),
            pltpu.SemaphoreType.DMA((gb, halves)),
            pltpu.SemaphoreType.DMA((gb, halves)),
            pltpu.VMEM(joined_gates.shape, jnp.float32),
            pltpu.SemaphoreType.DMA((4,)),
        ],
        compiler_params=pltpu.CompilerParams(
            collective_id=0, has_side_effects=True, vmem_limit_bytes=60 * 1024 * 1024
        ),
    )(values, joined_gates, pair_gate, layout_in, layout_out, gate_qubits, spare_values)
    return out.reshape(amplitudes.shape)


def solution(mesh):
    in_specs = (P(None, "grp", "dev", None), P(), P(), P(), P(), P(), P())
    out_specs = P(None, "grp", "dev", None)
    return jax.shard_map(
        per_device, mesh=mesh, in_specs=in_specs, out_specs=out_specs, check_vma=False
    )
```
